32 devices in a mesh: row: 4 (over z), col: 2 (over x), rep: 4 (over y, core).
Axes of the slice: x: 2, y: 2, z: 4, core: 2. Of those that a mesh axis runs over, the one named last changes fastest.
Arguments:
- tokens_in: bfloat16 [1024, 12288], P(('col', 'rep'), 'row'), may hold values from -6 to 6
- w_up: bfloat16 [12288, 24576], P('row', ('col', 'rep')), may hold values from -0.0546875 to 0.0546875
- w_down: bfloat16 [24576, 12288], P(('col', 'rep'), 'row'), may hold values from -0.0390625 to 0.0390625
- grad_out: bfloat16 [1024, 12288], P(('col', 'rep'), 'row'), may hold values from -6 to 6
Outputs:
- output: bfloat16 [1024, 12288], P(('col', 'rep'), 'row')
- grad_tokens: bfloat16 [1024, 12288], P(('col', 'rep'), 'row')
- grad_w_up: bfloat16 [12288, 24576], P('row', ('col', 'rep'))
- grad_w_down: bfloat16 [24576, 12288], P(('col', 'rep'), 'row')
The draws below stay inside these ranges and needn't reach their ends.
All inputs are finite; a program needn't handle non-finite values.
Results may differ from the reference program's by a relative error of at most 0.0049.
Values may be sent and summed in bfloat16 or wider, within the bound.
A program may use at most 192 MiB of HBM per device.

```python
import jax
import jax.numpy as jnp
from jax import lax

D = 12288
FF = 24576
TOK = 1024


def level_of(stream_key, dims, shards, low, top_value):
    def one(axis_at, shards_of):
        steps = jax.random.uniform(jax.random.fold_in(jax.random.fold_in(stream_key, 6), axis_at), (shards_of,), jnp.float32, low / len(shards), top_value / len(shards))
        return jnp.repeat(jnp.exp(steps), dims[axis_at] // shards_of).reshape((-1,) + (1,) * (len(dims) - axis_at - 1))

    level = one(*shards[0])
    for cut in shards[1:]:
        level = level * one(*cut)
    return level


def gaussian(own_key, dims, scale, most, split=(), kind=jnp.bfloat16):
    drawn = jax.random.normal(own_key, dims, jnp.float32) * scale
    if len(split) > 0:
        drawn = level_of(own_key, dims, split, -0.22, 0.18) * drawn
    return jnp.clip(drawn, min=-most, max=most).astype(kind)


def setup_inputs(seed: int = 0) -> dict:
    seeds = jax.random.split(jax.random.key(seed), 5)
    tokens_in = gaussian(seeds[0], (TOK, D), 1.0, 6.0, ((0, 8), (1, 4)))
    w_up = gaussian(seeds[1], (D, FF), D ** -0.5, 0.0546875, ((0, 4), (1, 8)))
    w_down = gaussian(seeds[2], (FF, D), FF ** -0.5, 0.0390625, ((0, 8), (1, 4)))
    grad_out = gaussian(seeds[3], (TOK, D), 1.0, 6.0, ((0, 8), (1, 4)))
    return dict(tokens_in=tokens_in, w_up=w_up, w_down=w_down, grad_out=grad_out)


def reference(tokens_in, w_up, w_down, grad_out):
    hidden = jnp.dot(tokens_in, w_up, preferred_element_type=jnp.float32)
    normal_cdf = 0.5 * (1.0 + lax.erf(hidden * 0.7071067811865476))
    activ = (hidden * normal_cdf).astype(jnp.bfloat16)
    output = jnp.dot(activ, w_down, preferred_element_type=jnp.float32).astype(jnp.bfloat16)
    grad_activ = jnp.dot(grad_out, w_down.T, preferred_element_type=jnp.float32)
    density = jnp.exp(-0.5 * hidden * hidden) * 0.3989422804014327
    grad_hidden = (grad_activ * (normal_cdf + hidden * density)).astype(jnp.bfloat16)
    token_scale = TOK ** -0.5
    grad_w_down = (jnp.dot(activ.T, grad_out, preferred_element_type=jnp.float32) * token_scale).astype(jnp.bfloat16)
    grad_w_up = (jnp.dot(tokens_in.T, grad_hidden, preferred_element_type=jnp.float32) * token_scale).astype(jnp.bfloat16)
    grad_tokens = jnp.dot(grad_hidden, w_up.T, preferred_element_type=jnp.float32).astype(jnp.bfloat16)
    return output, grad_tokens, grad_w_up, grad_w_down
```

```python
import jax
import jax.numpy as jnp
from jax import lax
from jax.sharding import PartitionSpec as P

TOKEN_AXES = ("col", "rep")
BF16 = jnp.bfloat16


def product(left_rows, weight, transposed):
    weight_dim = 1 if transposed else 0
    return lax.dot_general(
        left_rows, weight, (((1,), (weight_dim,)), ((), ())), preferred_element_type=jnp.float32
    )


def swap(block, distance):
    count = lax.axis_size(TOKEN_AXES)
    return lax.ppermute(block, TOKEN_AXES, [(i, i ^ distance) for i in range(count)])


def gather_chunks(block):
    chunks = []
    for distance in range(0, lax.axis_size(TOKEN_AXES), 2):
        first = block if distance == 0 else swap(block, distance)
        chunks.append(jnp.concatenate([first, swap(first, 1)], axis=0))
    return chunks


def pick(options, index):
    chosen = options[-1]
    for at in range(len(options) - 2, -1, -1):
        chosen = jnp.where(index == at, options[at], chosen)
    return chosen


def run_line(terms, finish):
    size, at, count = lax.axis_size("row"), lax.axis_index("row"), len(terms)
    half = size // 2
    lower = at < half
    depth = jnp.minimum(at, size - 1 - at)
    nothing = jnp.zeros(terms[0].shape, BF16)
    from_end, outward, finals = nothing, nothing, []
    for tick in range(count + size - 2):
        own = [terms[min(max(tick - k, 0), count - 1)] for k in range(half)]
        inward = pick(own, depth) + from_end.astype(jnp.float32)
        sent = inward.astype(BF16)
        busy = [i for i in range(size - 1) if 0 <= tick - i < count]
        right = lax.ppermute(
            jnp.where(lower, sent, outward), "row", [(i, i + 1) for i in busy]
        )
        left = lax.ppermute(
            jnp.where(lower, outward, sent), "row", [(size - 1 - i, size - 2 - i) for i in busy]
        )
        from_end = jnp.where(lower, right, left)
        outward = jnp.where(lower, left, right)
        term_at = tick - (half - 1)
        if 0 <= term_at < count:
            finished = finish(term_at, inward + outward.astype(jnp.float32))
            outward = jnp.where(depth == half - 1, finished, outward)
        finals.append(outward)
    return [
        pick([finals[u + size - 2 - k] for k in range(half)], depth) for u in range(count)
    ]


def sum_chunks(terms):
    total = None
    for at, term in enumerate(terms):
        rows = term.shape[0] // 2
        pair = term[:rows] + swap(term[rows:], 1)
        if at > 0:
            pair = swap(pair.astype(BF16), 2 * at).astype(jnp.float32)
        total = pair if total is None else total + pair
    return total.astype(BF16)


def gelu_parts(hidden):
    normal_cdf = 0.5 * (1.0 + lax.erf(hidden * 0.7071067811865476))
    density = jnp.exp(-0.5 * hidden * hidden) * 0.3989422804014327
    return (normal_cdf, density)


def on_device(tokens_in, w_up, w_down, grad_out):
    token_chunks = gather_chunks(tokens_in)
    grad_chunks = gather_chunks(grad_out)
    token_scale = (tokens_in.shape[0] * lax.axis_size(TOKEN_AXES)) ** (-0.5)
    chunk_count, rows = len(token_chunks), tokens_in.shape[0]
    terms = [product(chunk, w_up, False) for chunk in token_chunks]
    terms += [product(chunk, w_down, True) for chunk in grad_chunks]

    def run_half(first_row):
        slopes = []

        def finish(term_at, total):
            if term_at >= chunk_count:
                return (total * slopes[term_at - chunk_count]).astype(BF16)
            normal_cdf, density = gelu_parts(total)
            slopes.append(normal_cdf + total * density)
            return (total * normal_cdf).astype(BF16)

        return run_line([term[first_row : first_row + rows] for term in terms], finish)

    finals = [
        jnp.concatenate(pair, axis=0) for pair in zip(run_half(0), run_half(rows))
    ]
    activs, grads = finals[:chunk_count], finals[chunk_count:]
    output = sum_chunks([product(activ, w_down, False) for activ in activs])
    grad_tokens = sum_chunks([product(grad, w_up, True) for grad in grads])
    contract_rows = (((0,), (0,)), ((), ()))

    def weight_grad(left, right):
        summed = lax.dot_general(
            jnp.concatenate(left, axis=0),
            jnp.concatenate(right, axis=0),
            contract_rows,
            preferred_element_type=jnp.float32,
        )
        return (summed * token_scale).astype(BF16)

    grad_w_down = weight_grad(activs, grad_chunks)
    grad_w_up = weight_grad(token_chunks, grads)
    return (output, grad_tokens, grad_w_up, grad_w_down)


def solution(mesh):
    return jax.shard_map(
        on_device,
        mesh=mesh,
        in_specs=(
            P(("col", "rep"), "row"),
            P("row", ("col", "rep")),
            P(("col", "rep"), "row"),
            P(("col", "rep"), "row"),
        ),
        out_specs=(
            P(("col", "rep"), "row"),
            P(("col", "rep"), "row"),
            P("row", ("col", "rep")),
            P(("col", "rep"), "row"),
        ),
        check_vma=False,
    )
```
